128 devices in a mesh: row: 16 (over x, y_hi, core), col: 8 (over y_lo, z).
Axes of the slice: x: 4, y: 4 (y_hi: 2, y_lo: 2; y = y_hi * 2 + y_lo), z: 4, core: 2. Of those that a mesh axis runs over, the one named last changes fastest.
Arguments:
- inputs: bfloat16 [1024, 8192], P('col', 'row'), may hold values from -6 to 6
- cotangent: bfloat16 [1024, 8192], P('col', 'row'), may hold values from -1.5 to 1.5
- gate_weight: bfloat16 [8192, 14336], P('row', 'col'), may hold values from -0.0625 to 0.0625
- up_weight: bfloat16 [8192, 14336], P('row', 'col'), may hold values from -0.0625 to 0.0625
- down_weight: bfloat16 [14336, 8192], P('col', 'row'), may hold values from -0.046875 to 0.046875
Outputs:
- grad_inputs: bfloat16 [1024, 8192], P('col', 'row')
- grad_gate: bfloat16 [8192, 14336], P('row', 'col')
- grad_up: bfloat16 [8192, 14336], P('row', 'col')
- grad_down: bfloat16 [14336, 8192], P('col', 'row')
The draws below stay inside these ranges and needn't reach their ends.
All inputs are finite; a program needn't handle non-finite values.
Results may differ from the reference program's by a relative error of at most 0.015.
Values may be sent and summed in bfloat16 or wider, within the bound.
A program may use at most 128 MiB of HBM per device.

```python
import jax
import jax.numpy as jnp
from jax import lax

D = 8192
FF = 14336
TOKENS = 1024


def spiked(entries, own_key, source, target, blocks, factor):
    def block_of(dim):
        return (jnp.arange(entries.shape[dim]) // (entries.shape[dim] // blocks)).reshape((-1,) + (1,) * (entries.ndim - 1 - dim))

    near = jax.random.permutation(own_key, blocks)[block_of(target)]
    far = (block_of(target) + blocks // 2) % blocks
    return jnp.where((block_of(source) == near) | (block_of(source) == far), factor * entries, entries)


def shard_levels(own_key, shape, pieces, smallest, high):
    def one(axis_at, parts):
        steps = jax.random.uniform(jax.random.fold_in(jax.random.fold_in(own_key, 6), axis_at), (parts,), jnp.float32, smallest / len(pieces), high / len(pieces))
        return jnp.repeat(jnp.exp(steps), shape[axis_at] // parts).reshape((-1,) + (1,) * (len(shape) - axis_at - 1))

    gain = one(*pieces[0])
    for cut in pieces[1:]:
        gain = gain * one(*cut)
    return gain


def normal_values(own_key, extent, deviation, limit, cuts=(), dtype=jnp.bfloat16):
    factor_of = shard_levels(own_key, extent, cuts, -0.22, 0.18) if cuts else 1.0
    values = jax.random.normal(own_key, extent, jnp.float32) * deviation * factor_of
    return jnp.minimum(jnp.maximum(values, -limit), limit).astype(dtype)


def noise_with(key, dims, scale, bound, pieces, heavy, dtype=jnp.bfloat16):
    array = scale * jax.random.normal(key, dims, jnp.float32)
    if pieces:
        array = array * shard_levels(key, dims, pieces, -0.22, 0.18)
    return jnp.clip(spiked(array, jax.random.fold_in(key, 3), *heavy), -bound, bound).astype(dtype)


def setup_inputs(seed: int = 0) -> dict:
    seeds = jax.random.split(jax.random.key(seed), 6)
    return {
        "inputs": noise_with(seeds[0], (TOKENS, D), 1.0, 6.0, ((0, 8), (1, 16)), (1, 0, 16, 2.0)),
        "cotangent": noise_with(seeds[1], (TOKENS, D), 0.25, 1.5, ((0, 8), (1, 16)), (1, 0, 16, 2.0)),
        "gate_weight": normal_values(seeds[2], (D, FF), D ** -0.5, 0.0625, ((0, 16), (1, 8))),
        "up_weight": normal_values(seeds[3], (D, FF), D ** -0.5, 0.0625, ((0, 16), (1, 8))),
        "down_weight": normal_values(seeds[4], (FF, D), FF ** -0.5, 0.046875, ((0, 8), (1, 16))),
    }


def contract_first(left_side, right_side):
    return lax.dot_general(left_side, right_side, (((0,), (0,)), ((), ())), preferred_element_type=jnp.float32)


def contract_last(left_side, right_side):
    return lax.dot_general(left_side, right_side, (((1,), (1,)), ((), ())), preferred_element_type=jnp.float32)


def reference(inputs, cotangent, gate_weight, up_weight, down_weight):
    gate = jnp.dot(inputs, gate_weight, preferred_element_type=jnp.float32).astype(jnp.bfloat16)
    up_value = jnp.dot(inputs, up_weight, preferred_element_type=jnp.float32).astype(jnp.bfloat16)
    gate_val = gate.astype(jnp.float32)
    up_val = up_value.astype(jnp.float32)
    sigmoid_gate = jax.nn.sigmoid(gate_val)
    activated = gate_val * sigmoid_gate
    hidden = (activated * up_val).astype(jnp.bfloat16)
    hidden_grad = contract_last(cotangent, down_weight).astype(jnp.bfloat16)
    grad_down = contract_first(hidden, cotangent).astype(jnp.bfloat16)
    grad_val = hidden_grad.astype(jnp.float32)
    gate_grad = (grad_val * up_val * sigmoid_gate * (1.0 + gate_val * (1.0 - sigmoid_gate))).astype(jnp.bfloat16)
    up_grad = (grad_val * activated).astype(jnp.bfloat16)
    grad_gate = contract_first(inputs, gate_grad).astype(jnp.bfloat16)
    grad_up = contract_first(inputs, up_grad).astype(jnp.bfloat16)
    grad_inputs = (contract_last(gate_grad, gate_weight) + contract_last(up_grad, up_weight)).astype(jnp.bfloat16)
    return grad_inputs, grad_gate, grad_up, grad_down
```

```python
import jax
import jax.numpy as jnp
from jax import lax
from jax.experimental import pallas as pl
from jax.experimental.pallas import tpu as pltpu
from jax.sharding import PartitionSpec as P

MESH = pl.DeviceIdType.MESH
BLOCKS = 8
STEPS = 8
CORE, FIRST, SECOND, FAR, FAR_BACK, SECOND_BACK, FIRST_BACK, CORE_BACK = range(STEPS)
NT = (((1,), (1,)), ((), ()))
TN = (((0,), (0,)), ((), ()))


def dot(a, b, dims=(((1,), (0,)), ((), ()))):
    return lax.dot_general(a, b, dims, preferred_element_type=jnp.float32)


def kernel(
    x_in, y_in, gate_in, up_in, down_in,
    gx_out, gg_out, gu_out, gd_out,
    xs, ys, wg, wu, wd, part, r_core, r_first, r_second, r_far, full, acc_gate, acc_up, acc_down,
    dx_send, dx_recv, dx_out, local_sem, send_sem, recv_sem, col_send, col_recv, dx_ssem, dx_rsem,
):
    rows = x_in.shape[0]
    width = x_in.shape[1]
    half = gate_in.shape[1] // 2
    n1, n2, n3 = rows // 2, rows // 4, rows // 8
    row, col = lax.axis_index("row"), lax.axis_index("col")
    core, y_hi, x = row % 2, (row // 2) % 2, row // 4
    y_lo, z = col // 4, col % 4
    bit_a, bit_b = x // 2, (x + x // 2) % 2
    flip_a, flip_b = 3 - x, x + 1 - 2 * (x % 2)
    keep1 = core * bit_a + (1 - core) * bit_b
    keep2 = core * bit_b + (1 - core) * bit_a
    x1 = core * flip_a + (1 - core) * flip_b
    x2 = core * flip_b + (1 - core) * flip_a
    sibling = (row + 1 - 2 * core, col)
    first = (x1 * 4 + y_hi * 2 + core, col)
    second = (x2 * 4 + y_hi * 2 + core, col)
    far = (x * 4 + (1 - y_hi) * 2 + core, col)
    k1 = keep1 * n1
    k2 = k1 + keep2 * n2
    k3 = k2 + y_hi * n3

    def at_col(step, sign):
        dy, dz = step // 4, step % 4
        return (row, (y_lo + dy - 2 * y_lo * dy) * 4 + (z + sign * dz + 4) % 4)

    def span(start, size):
        return pl.ds(pl.multiple_of(start, n3), size)

    def block(s):
        return pl.ds(pl.multiple_of(s * rows, rows), rows)

    def remote(step, s, m):
        if step == CORE:
            src, dst, dev = part.at[s, m, 1 - core], r_core.at[s, m], sibling
        elif step == FIRST:
            src, dst, dev = part.at[s, m, core, span((1 - keep1) * n1, n1)], r_first.at[s, m], first
        elif step == SECOND:
            src = part.at[s, m, core, span(k1 + (1 - keep2) * n2, n2)]
            dst, dev = r_second.at[s, m], second
        elif step == FAR:
            src = part.at[s, m, core, span(k2 + (1 - y_hi) * n3, n3)]
            dst, dev = r_far.at[s, m], far
        else:
            start, size, dev = {
                FAR_BACK: (k3, n3, far),
                SECOND_BACK: (k2, n2, second),
                FIRST_BACK: (k1, n1, first),
                CORE_BACK: (0, rows, sibling),
            }[step]
            src = dst = full.at[m, core, span(s * rows + start, size)]
        return pltpu.make_async_remote_copy(
            src_ref=src,
            dst_ref=dst,
            send_sem=send_sem.at[step, s, m],
            recv_sem=recv_sem.at[step, s, m],
            device_id=dev,
            device_id_type=MESH,
        )

    def column(which, s):
        ref = (xs, ys)[which]
        return pltpu.make_async_remote_copy(
            src_ref=ref.at[pl.ds(0, rows)],
            dst_ref=ref.at[block(s)],
            send_sem=col_send.at[which, s],
            recv_sem=col_recv.at[which, s],
            device_id=at_col(s, -1),
            device_id_type=MESH,
        )

    def dx_copy(s):
        return pltpu.make_async_remote_copy(
            src_ref=dx_send.at[s],
            dst_ref=dx_recv.at[s],
            send_sem=dx_ssem.at[s],
            recv_sem=dx_rsem.at[s],
            device_id=at_col(s, 1),
            device_id_type=MESH,
        )

    def load(i, src, dst):
        return pltpu.make_async_copy(src, dst, local_sem.at[i])

    loads = [
        load(0, x_in, xs.at[pl.ds(0, rows)]),
        load(1, y_in, ys.at[pl.ds(0, rows)]),
        load(2, gate_in, wg),
        load(3, up_in, wu),
        load(4, down_in, wd),
    ]
    for copy in loads:
        copy.start()

    barrier = pltpu.get_barrier_semaphore()
    partners = [sibling, first, second, far] + [at_col(s, 1) for s in range(1, BLOCKS)]
    for dev in partners:
        pl.semaphore_signal(barrier, inc=1, device_id=dev, device_id_type=MESH)
    pl.semaphore_wait(barrier, len(partners))

    loads[0].wait()
    loads[1].wait()
    for s in range(1, BLOCKS):
        column(0, s).start()
        column(1, s).start()
    for copy in loads[2:]:
        copy.wait()

    def f32(v):
        return v.astype(jnp.float32)

    def partials(s):
        @pl.when(s > 0)
        def _():
            column(0, s).wait_recv()
            column(1, s).wait_recv()

        for m in range(3):
            for h in range(2):
                if m < 2:
                    value = dot(xs[block(s), :], (wg, wu)[m][:, h * half : (h + 1) * half])
                else:
                    value = dot(ys[block(s), :], wd[h * half : (h + 1) * half, :], NT)
                part[s, m, h] = value.astype(jnp.bfloat16)
            remote(CORE, s, m).start()

    def send_first(s):
        for m in range(3):
            remote(CORE, s, m).wait_recv()
            q = span((1 - keep1) * n1, n1)
            total = f32(part[s, m, core, q, :]) + f32(r_core[s, m, q, :])
            part[s, m, core, q, :] = total.astype(jnp.bfloat16)
            remote(FIRST, s, m).start()

    def send_second(s):
        for m in range(3):
            remote(FIRST, s, m).wait_recv()
            o = (1 - keep2) * n2
            q = span(k1 + o, n2)
            total = (
                f32(part[s, m, core, q, :])
                + f32(r_core[s, m, q, :])
                + f32(r_first[s, m, span(o, n2), :])
            )
            part[s, m, core, q, :] = total.astype(jnp.bfloat16)
            remote(SECOND, s, m).start()

    def send_far(s):
        for m in range(3):
            remote(SECOND, s, m).wait_recv()
            o = (1 - y_hi) * n3
            q = span(k2 + o, n3)
            total = (
                f32(part[s, m, core, q, :])
                + f32(r_core[s, m, q, :])
                + f32(r_first[s, m, span(keep2 * n2 + o, n3), :])
                + f32(r_second[s, m, span(o, n3), :])
            )
            part[s, m, core, q, :] = total.astype(jnp.bfloat16)
            remote(FAR, s, m).start()

    def activate(s):
        q = span(k3, n3)
        sums = []
        for m in range(3):
            remote(FAR, s, m).wait_recv()
            total = (
                f32(part[s, m, core, q, :])
                + f32(r_core[s, m, q, :])
                + f32(r_first[s, m, span(keep2 * n2 + y_hi * n3, n3), :])
                + f32(r_second[s, m, span(y_hi * n3, n3), :])
                + f32(r_far[s, m])
            )
            sums.append(f32(total.astype(jnp.bfloat16)))
        gate, up, grad = sums
        sig = 1.0 / (1.0 + jnp.exp(-gate))
        act = gate * sig
        out = (act * up, grad * up * sig * (1.0 + gate * (1.0 - sig)), grad * act)
        for m in range(3):
            full[m, core, span(s * rows + k3, n3), :] = out[m].astype(jnp.bfloat16)
            remote(FAR_BACK, s, m).start()

    def forward(step, s):
        for m in range(3):
            remote(step - 1, s, m).wait_recv()
            remote(step, s, m).start()

    def input_grad(s):
        for m in range(3):
            remote(CORE_BACK, s, m).wait_recv()
        total = None
        for m, w in ((1, wg), (2, wu)):
            for h in range(2):
                term = dot(full[m, h, block(s), :], w[:, h * half : (h + 1) * half], NT)
                total = term if total is None else total + term
        value = total.astype(jnp.bfloat16)

        @pl.when(s == 0)
        def _():
            dx_recv[0] = value

        @pl.when(s > 0)
        def _():
            dx_send[s] = value
            dx_copy(s).start()

    def weight_grads(start, depth, opening, closing):
        tokens = pl.ds(start, depth)

        def put(acc, out, at, value):
            if not opening:
                value = value + acc[at]
            if closing:
                out[at] = value.astype(jnp.bfloat16)
            else:
                acc[at] = value

        tile = 128
        for m, acc, out in ((1, acc_gate, wg), (2, acc_up, wu)):
            for h in range(2):

                @pl.loop(0, width // tile)
                def _(i):
                    r = pl.ds(pl.multiple_of(i * tile, tile), tile)
                    value = dot(xs[tokens, r], full[m, h, tokens, :], TN)
                    put(acc, out, (r, slice(h * half, (h + 1) * half)), value)

        for h in range(2):

            @pl.loop(0, half // tile)
            def _(i):
                r = pl.ds(pl.multiple_of(i * tile, tile), tile)
                value = dot(full[0, h, tokens, r], ys[tokens, :], TN)
                put(acc_down, wd, (pl.ds(pl.multiple_of(h * half + i * tile, tile), tile), slice(None)), value)

    def on(t, delay, step):
        @pl.when((t >= delay) & (t < delay + BLOCKS))
        def _():
            step(t - delay)

    last = BLOCKS + 7

    @pl.loop(0, last + 1)
    def _(t):
        on(t, 2, send_second)
        on(t, 3, send_far)
        on(t, 4, activate)
        on(t, 5, lambda s: forward(SECOND_BACK, s))
        on(t, 6, lambda s: forward(FIRST_BACK, s))
        on(t, 7, lambda s: forward(CORE_BACK, s))
        on(t, 0, partials)
        on(t, 1, send_first)
        on(t, 8, input_grad)

        @pl.when(t == 8 + 3)
        def _():
            weight_grads(0, 4 * rows, True, False)

        @pl.when(t == 8 + 5)
        def _():
            weight_grads(4 * rows, 2 * rows, False, False)

    weight_grads(6 * rows, 2 * rows, False, True)
    stores = [load(0, wg, gg_out), load(1, wu, gu_out), load(2, wd, gd_out)]
    for copy in stores:
        copy.start()
    total = f32(dx_recv[0])
    for s in range(1, BLOCKS):
        dx_copy(s).wait_recv()
        total = total + f32(dx_recv[s])
    dx_out[...] = total.astype(jnp.bfloat16)
    store = load(3, dx_out, gx_out)
    store.start()

    @pl.loop(0, BLOCKS)
    def _(s):
        for step in range(STEPS):
            for m in range(3):
                remote(step, s, m).wait_send()

    for s in range(1, BLOCKS):
        column(0, s).wait_send()
        column(1, s).wait_send()
        dx_copy(s).wait_send()
    for copy in stores:
        copy.wait()
    store.wait()


def on_device(inputs, cotangent, gate_weight, up_weight, down_weight):
    rows, width = inputs.shape
    columns = gate_weight.shape[1]
    half, tokens = columns // 2, rows * BLOCKS
    bf16, f32 = jnp.bfloat16, jnp.float32
    anywhere = pl.BlockSpec(memory_space=pl.ANY)
    dma = pltpu.SemaphoreType.DMA
    return pl.pallas_call(
        kernel,
        out_shape=[
            jax.ShapeDtypeStruct(a.shape, bf16) for a in (inputs, gate_weight, up_weight, down_weight)
        ],
        in_specs=[anywhere] * 5,
        out_specs=[anywhere] * 4,
        scratch_shapes=[
            pltpu.VMEM((tokens, width), bf16),
            pltpu.VMEM((tokens, width), bf16),
            pltpu.VMEM((width, columns), bf16),
            pltpu.VMEM((width, columns), bf16),
            pltpu.VMEM((columns, width), bf16),
            pltpu.VMEM((BLOCKS, 3, 2, rows, half), bf16),
            pltpu.VMEM((BLOCKS, 3, rows, half), bf16),
            pltpu.VMEM((BLOCKS, 3, rows // 2, half), bf16),
            pltpu.VMEM((BLOCKS, 3, rows // 4, half), bf16),
            pltpu.VMEM((BLOCKS, 3, rows // 8, half), bf16),
            pltpu.VMEM((3, 2, tokens, half), bf16),
            pltpu.VMEM((width, columns), f32),
            pltpu.VMEM((width, columns), f32),
            pltpu.VMEM((columns, width), f32),
            pltpu.VMEM((BLOCKS, rows, width), bf16),
            pltpu.VMEM((BLOCKS, rows, width), bf16),
            pltpu.VMEM((rows, width), bf16),
            dma((5,)),
            dma((STEPS, BLOCKS, 3)),
            dma((STEPS, BLOCKS, 3)),
            dma((2, BLOCKS)),
            dma((2, BLOCKS)),
            dma((BLOCKS,)),
            dma((BLOCKS,)),
        ],
        compiler_params=pltpu.CompilerParams(
            collective_id=0, has_side_effects=True, vmem_limit_bytes=62 * 1024 * 1024
        ),
        cost_estimate=pl.CostEstimate(
            flops=16 * tokens * width * columns, bytes_accessed=24_000_000, transcendentals=0
        ),
    )(inputs, cotangent, gate_weight, up_weight, down_weight)


def solution(mesh):
    placed = (P("col", "row"), P("col", "row"), P("row", "col"), P("row", "col"), P("col", "row"))
    return jax.shard_map(
        on_device,
        mesh=mesh,
        in_specs=placed,
        out_specs=(P("col", "row"), P("row", "col"), P("row", "col"), P("col", "row")),
        check_vma=False,
    )
```

```python
import jax
import jax.numpy as jnp
from jax import lax
from jax.experimental import pallas as pl
from jax.experimental.pallas import tpu as pltpu
from jax.sharding import PartitionSpec as P

MESH = pl.DeviceIdType.MESH
BLOCKS = 8
OFFSETS = ((0, 0), (0, 1), (1, 0), (0, 3), (1, 1), (1, 3), (0, 2), (1, 2))
SENDS = {1: (0, 1), 2: (0, 0), 3: (0, 3), 4: (2, 1), 5: (2, 3), 6: (0, 2), 7: (2, 2)}
SEND_AT = {1: (6,), 2: (4, 5), 3: (7,)}
DELAYS = (0, 1, 3, 5, 7, 9, 11, 14, 16)
ORDER = (1, 5, 8, 6, 3, 2, 0, 4, 7)
FAR_FIRST = (2,)
NT = (((1,), (1,)), ((), ()))
TN = (((0,), (0,)), ((), ()))


def dot(a, b, dims=(((1,), (0,)), ((), ()))):
    return lax.dot_general(a, b, dims, preferred_element_type=jnp.float32)


def exchange_kernel(
    x_in, y_in, gate_in, up_in, down_in,
    gx_out, x_out, y_out, full_out,
    xs, ys, wg, wu, wd, part, r_core, r_one, r_two, r_three, full,
    dx_send, dx_recv, dx_out, local_sem, send_sem, recv_sem, col_send, col_recv, dx_ssem, dx_rsem, out_sem,
):
    rows = x_in.shape[0]
    half = gate_in.shape[1] // 2
    shape = part.shape[3:]
    row, col = lax.axis_index("row"), lax.axis_index("col")
    core, y_hi, x = row % 2, (row // 2) % 2, row // 4
    y_lo, z = col // 4, col % 4
    bit_a, bit_b = x // 2, (x + x // 2) % 2
    flip_a, flip_b = 3 - x, x + 1 - 2 * (x % 2)
    i1 = core * bit_a + (1 - core) * bit_b
    i2 = core * bit_b + (1 - core) * bit_a
    i3 = y_hi
    x1 = core * flip_a + (1 - core) * flip_b
    x2 = core * flip_b + (1 - core) * flip_a
    sibling = (row + 1 - 2 * core, col)
    first = (x1 * 4 + y_hi * 2 + core, col)
    second = (x2 * 4 + y_hi * 2 + core, col)
    far = (x * 4 + (1 - y_hi) * 2 + core, col)
    every = slice(None)

    def at_col(k, sign):
        dy, dz = OFFSETS[k]
        return (row, (1 - y_lo if dy else y_lo) * 4 + (z + sign * dz + 4) % 4)

    def leaving(m):
        if m in FAR_FIRST:
            return (far, (every, every, 1 - i3)), (first, (1 - i1, every, i3)), (second, (i1, 1 - i2, i3))
        return (first, (1 - i1,)), (second, (i1, 1 - i2)), (far, (i1, i2, 1 - i3))

    def returning(m):
        if m in FAR_FIRST:
            return (second, (i1, i2, i3)), (first, (i1, every, i3)), (far, (every, every, i3))
        return (far, (i1, i2, i3)), (second, (i1, i2)), (first, (i1,))

    def kept(m):
        if m in FAR_FIRST:
            return ((1 - i1,),), ((i1, 1 - i2), (1 - i2,)), ((i1, i2), (i2,))
        return ((1 - i2,),), ((i2, 1 - i3), (1 - i3,)), ((i2, i3), (i3,))

    def remote(step, s, m):
        if step == 0:
            src, dst, dev = part.at[s, m, 1 - core], r_core.at[s, m], sibling
        elif step < 4:
            dev, place = leaving(m)[step - 1]
            src, dst = part.at[(s, m, core) + place], (r_one, r_two, r_three)[step - 1].at[s, m]
        else:
            dev, place = (sibling, ()) if step == 7 else returning(m)[step - 4]
            src = dst = full.at[(m, core, s) + place]
        return pltpu.make_async_remote_copy(
            src_ref=src,
            dst_ref=dst,
            send_sem=send_sem.at[step, s, m],
            recv_sem=recv_sem.at[step, s, m],
            device_id=dev,
            device_id_type=MESH,
        )

    def column(which, k, s=None):
        source, dz = SENDS.get(k, (0, 1))
        ref = (xs, ys)[which]
        target = at_col(k, -1) if source == 0 else (row, y_lo * 4 + (z - OFFSETS[k][1] + 4) % 4)
        slot = k if s is None else s
        return pltpu.make_async_remote_copy(
            src_ref=ref.at[pl.ds(source * rows, rows)],
            dst_ref=ref.at[pl.ds(pl.multiple_of(slot * rows, rows), rows)],
            send_sem=col_send.at[which, slot],
            recv_sem=col_recv.at[which, slot],
            device_id=target,
            device_id_type=MESH,
        )

    def dx_copy(k):
        return pltpu.make_async_remote_copy(
            src_ref=dx_send.at[k],
            dst_ref=dx_recv.at[k],
            send_sem=dx_ssem.at[k],
            recv_sem=dx_rsem.at[k],
            device_id=at_col(k, 1),
            device_id_type=MESH,
        )

    def local(i, src, dst):
        return pltpu.make_async_copy(src, dst, local_sem.at[i])

    def save(s, m, h):
        columns = slice(h * half, (h + 1) * half)
        return pltpu.make_async_copy(
            full.at[m, h, s], full_out.at[m, s, :, :, :, :, columns], out_sem.at[s, m, h]
        )

    loads = [
        local(0, x_in, xs.at[pl.ds(0, rows)]),
        local(1, y_in, ys.at[pl.ds(0, rows)]),
        local(2, gate_in, wg),
        local(3, up_in, wu),
        local(4, down_in, wd),
    ]
    for copy in loads:
        copy.start()

    barrier = pltpu.get_barrier_semaphore()
    partners = [sibling, first, second, far] + [at_col(k, 1) for k in range(1, BLOCKS)]
    for dev in partners:
        pl.semaphore_signal(barrier, inc=1, device_id=dev, device_id_type=MESH)
    pl.semaphore_wait(barrier, len(partners))

    for which in range(2):
        loads[which].wait()
        for k in (1, 2, 3):
            column(which, k).start()
    for copy in loads[2:]:
        copy.wait()

    def f32(v):
        return v.astype(jnp.float32)

    def gathered(which, s):
        @pl.when(s > 0)
        def _():
            column(which, 1, s).wait_recv()

        for at, ks in SEND_AT.items():

            @pl.when(s == at)
            def _():
                for k in ks:
                    column(which, k).start()

    def partials(s):
        block = pl.ds(pl.multiple_of(s * rows, rows), rows)
        for m in range(3):
            if m != 1:
                gathered(m // 2, s)
            for h in range(2):
                if m < 2:
                    value = dot(xs[block, :], (wg, wu)[m][:, h * half : (h + 1) * half])
                else:
                    value = dot(ys[block, :], wd[h * half : (h + 1) * half, :], NT)
                part[s, m, h] = value.astype(jnp.bfloat16).reshape(shape)
            remote(0, s, m).start()

    def reduce(step, s):
        for m in range(3):
            remote(step - 1, s, m).wait_recv()
            place = leaving(m)[step - 1][1]
            total = f32(part[(s, m, core) + place]) + f32(r_core[(s, m) + place])
            if step > 1:
                for ref, at in zip((r_one, r_two), kept(m)[step - 2]):
                    total = total + f32(ref[(s, m) + at])
            part[(s, m, core) + place] = total.astype(jnp.bfloat16)
            remote(step, s, m).start()

    def activate(s):
        sums = []
        for m in range(3):
            remote(3, s, m).wait_recv()
            total = f32(part[s, m, core, i1, i2, i3]) + f32(r_core[s, m, i1, i2, i3])
            for ref, at in zip((r_one, r_two), kept(m)[2]):
                total = total + f32(ref[(s, m) + at])
            total = total + f32(r_three[s, m])
            sums.append(f32(total.astype(jnp.bfloat16)))
        gate, up, grad = sums
        sig = 1.0 / (1.0 + jnp.exp(-gate))
        act = gate * sig
        out = (act * up, grad * up * sig * (1.0 + gate * (1.0 - sig)), grad * act)
        for m in range(3):
            full[m, core, s, i1, i2, i3] = out[m].astype(jnp.bfloat16)
            remote(4, s, m).start()

    def spread(step, s):
        for m in range(3):
            remote(step - 1, s, m).wait_recv()
            remote(step, s, m).start()

    def input_grad(s):
        for m in range(3):
            remote(7, s, m).wait_recv()
            for h in range(2):
                save(s, m, h).start()
        total = None
        for m, w in ((1, wg), (2, wu)):
            for h in range(2):
                values = full[m, h, s].reshape(rows, half)
                term = dot(values, w[:, h * half : (h + 1) * half], NT)
                total = term if total is None else total + term
        value = total.astype(jnp.bfloat16)

        @pl.when(s == 0)
        def _():
            dx_recv[0] = value

        @pl.when(s > 0)
        def _():
            dx_send[s] = value

        for k in range(1, BLOCKS):

            @pl.when(s == k)
            def _():
                dx_copy(k).start()

    def stage(number, s):
        if number == 0:
            partials(s)
        elif number < 4:
            reduce(number, s)
        elif number == 4:
            activate(s)
        elif number < 8:
            spread(number, s)
        else:
            input_grad(s)

    @pl.loop(0, BLOCKS + max(DELAYS))
    def _(t):
        for number in ORDER:
            delay = DELAYS[number]

            @pl.when((t >= delay) & (t < delay + BLOCKS))
            def _():
                stage(number, t - delay)

    stores = [local(0, xs, x_out), local(1, ys, y_out)]
    for copy in stores:
        copy.start()
    total = f32(dx_recv[0])
    for k in range(1, BLOCKS):
        dx_copy(k).wait_recv()
        total = total + f32(dx_recv[k])
    dx_out[...] = total.astype(jnp.bfloat16)
    stores.append(local(2, dx_out, gx_out))
    stores[-1].start()

    @pl.loop(0, BLOCKS)
    def _(s):
        for m in range(3):
            for step in range(8):
                remote(step, s, m).wait_send()
            for h in range(2):
                save(s, m, h).wait()

    for k in range(1, BLOCKS):
        column(0, k).wait_send()
        column(1, k).wait_send()
        dx_copy(k).wait_send()
    for copy in stores:
        copy.wait()


def weights_kernel(gx_in, x_ref, y_ref, full_ref, gx_out, gate_out, up_out, down_out):
    step = pl.program_id(0)
    values = full_ref[0]

    @pl.when(step == 0)
    def _():
        gx_out[...] = gx_in[...]

    for at, out in ((0, gate_out), (2, up_out)):

        @pl.when((step >= at) & (step < at + 2))
        def _():
            out[...] = dot(x_ref[...], values, TN).astype(jnp.bfloat16)

    @pl.when(step >= 4)
    def _():
        down_out[...] = dot(values, y_ref[...], TN).astype(jnp.bfloat16)


def on_device(inputs, cotangent, gate_weight, up_weight, down_weight):
    rows, width = inputs.shape
    columns = gate_weight.shape[1]
    half, tokens = columns // 2, rows * BLOCKS
    bf16 = jnp.bfloat16
    block = (2, 2, 2, rows // 8)
    anywhere = pl.BlockSpec(memory_space=pl.ANY)
    dma = pltpu.SemaphoreType.DMA
    gx, x_all, y_all, full = pl.pallas_call(
        exchange_kernel,
        out_shape=[
            jax.ShapeDtypeStruct((rows, width), bf16),
            jax.ShapeDtypeStruct((tokens, width), bf16),
            jax.ShapeDtypeStruct((tokens, width), bf16),
            jax.ShapeDtypeStruct((3, BLOCKS, *block, columns), bf16),
        ],
        in_specs=[anywhere] * 5,
        out_specs=[anywhere] * 4,
        scratch_shapes=[
            pltpu.VMEM((tokens, width), bf16),
            pltpu.VMEM((tokens, width), bf16),
            pltpu.VMEM((width, columns), bf16),
            pltpu.VMEM((width, columns), bf16),
            pltpu.VMEM((columns, width), bf16),
            pltpu.VMEM((BLOCKS, 3, 2, *block, half), bf16),
            pltpu.VMEM((BLOCKS, 3, *block, half), bf16),
            pltpu.VMEM((BLOCKS, 3, *block[1:], half), bf16),
            pltpu.VMEM((BLOCKS, 3, *block[2:], half), bf16),
            pltpu.VMEM((BLOCKS, 3, *block[3:], half), bf16),
            pltpu.VMEM((3, 2, BLOCKS, *block, half), bf16),
            pltpu.VMEM((BLOCKS, rows, width), bf16),
            pltpu.VMEM((BLOCKS, rows, width), bf16),
            pltpu.VMEM((rows, width), bf16),
            dma((5,)),
            dma((8, BLOCKS, 3)),
            dma((8, BLOCKS, 3)),
            dma((2, BLOCKS)),
            dma((2, BLOCKS)),
            dma((BLOCKS,)),
            dma((BLOCKS,)),
            dma((BLOCKS, 3, 2)),
        ],
        compiler_params=pltpu.CompilerParams(
            collective_id=0, has_side_effects=True, vmem_limit_bytes=56 * 1024 * 1024
        ),
        cost_estimate=pl.CostEstimate(
            flops=10 * tokens * width * columns, bytes_accessed=24_000_000, transcendentals=0
        ),
    )(inputs, cotangent, gate_weight, up_weight, down_weight)

    def whole(shape):
        return pl.BlockSpec(shape, lambda j: (0, 0))

    return pl.pallas_call(
        weights_kernel,
        grid=(6,),
        out_shape=[
            jax.ShapeDtypeStruct(a.shape, bf16) for a in (inputs, gate_weight, up_weight, down_weight)
        ],
        in_specs=[
            whole((rows, width)),
            whole((tokens, width)),
            whole((tokens, width)),
            pl.BlockSpec((1, tokens, half), lambda j: ((j // 2 + 1) % 3, 0, j % 2)),
        ],
        out_specs=[
            whole((rows, width)),
            pl.BlockSpec((width, half), lambda j: (0, jnp.minimum(j, 1))),
            pl.BlockSpec((width, half), lambda j: (0, jnp.clip(j - 2, 0, 1))),
            pl.BlockSpec((half, width), lambda j: (jnp.maximum(j - 4, 0), 0)),
        ],
        compiler_params=pltpu.CompilerParams(vmem_limit_bytes=56 * 1024 * 1024),
        cost_estimate=pl.CostEstimate(
            flops=6 * tokens * width * columns, bytes_accessed=20_000_000, transcendentals=0
        ),
    )(gx, x_all, y_all, full.reshape(3, tokens, columns))


def solution(mesh):
    placed = (P("col", "row"), P("col", "row"), P("row", "col"), P("row", "col"), P("col", "row"))
    return jax.shard_map(
        on_device,
        mesh=mesh,
        in_specs=placed,
        out_specs=(P("col", "row"), P("row", "col"), P("row", "col"), P("col", "row")),
        check_vma=False,
    )
```

```python
import itertools

import jax
import jax.numpy as jnp
from jax import lax
from jax.experimental import pallas as pl
from jax.experimental.pallas import tpu as pltpu
from jax.sharding import PartitionSpec as P

MESH = pl.DeviceIdType.MESH
BLOCKS = 8
OFFSETS = ((0, 0), (0, 1), (1, 0), (0, 3), (1, 1), (1, 3), (0, 2), (1, 2))
SENDS = {1: (0, 1), 2: (0, 0), 3: (0, 3), 4: (2, 1), 5: (2, 3), 6: (0, 2), 7: (2, 2)}
SEND_AT = {1: (4, 5), 2: (6,), 3: (7,)}
DELAYS = (0, 1, 4, 6, 9, 10, 13, 15, 16, 16)
ORDER = ((4, 0), (2, 0), (2, 1), (2, 2), (6, 0), (6, 1), (6, 2), (3, 0), (3, 1), (3, 2), (1, 0), (1, 1), (1, 2), (8, 0), (7, 0), (7, 1), (7, 2), (9, 0), (9, 1), (9, 2), (5, 0), (5, 1), (5, 2), (0, 0), (0, 1), (0, 2))
FAR_FIRST = (2,)
FAR_LAST = (2,)
NT = (((1,), (1,)), ((), ()))
TN = (((0,), (0,)), ((), ()))


def dot(a, b, dims=(((1,), (0,)), ((), ()))):
    return lax.dot_general(a, b, dims, preferred_element_type=jnp.float32)


def exchange_kernel(
    x_in, y_in, gate_in, up_in, down_in,
    gx_out, gate_out, up_out, down_out,
    xs, ys, wg, wu, wd, part, r_core, r_one, r_two, r_three, full, acc_gate, acc_up, acc_down,
    dx_send, dx_recv, local_sem, send_sem, recv_sem, col_send, col_recv, dx_ssem, dx_rsem,
):
    rows, width = x_in.shape
    half = gate_in.shape[1] // 2
    shape = part.shape[3:]
    row, col = lax.axis_index("row"), lax.axis_index("col")
    core, y_hi, x = row % 2, (row // 2) % 2, row // 4
    y_lo, z = col // 4, col % 4
    bit_a, bit_b = x // 2, (x + x // 2) % 2
    flip_a, flip_b = 3 - x, x + 1 - 2 * (x % 2)
    i1 = core * bit_a + (1 - core) * bit_b
    i2 = core * bit_b + (1 - core) * bit_a
    i3 = y_hi
    x1 = core * flip_a + (1 - core) * flip_b
    x2 = core * flip_b + (1 - core) * flip_a
    sibling = (row + 1 - 2 * core, col)
    first = (x1 * 4 + y_hi * 2 + core, col)
    second = (x2 * 4 + y_hi * 2 + core, col)
    far = (x * 4 + (1 - y_hi) * 2 + core, col)
    every = slice(None)

    def at_col(k, sign):
        dy, dz = OFFSETS[k]
        return (row, (1 - y_lo if dy else y_lo) * 4 + (z + sign * dz + 4) % 4)

    def leaving(m):
        if m in FAR_FIRST:
            return (far, (every, every, 1 - i3)), (first, (1 - i1, every, i3)), (second, (i1, 1 - i2, i3))
        return (first, (1 - i1,)), (second, (i1, 1 - i2)), (far, (i1, i2, 1 - i3))

    def returning(m):
        if m in FAR_LAST:
            return (second, (i1, i2, i3)), (first, (i1, every, i3)), (far, (every, every, i3))
        return (far, (i1, i2, i3)), (second, (i1, i2)), (first, (i1,))

    def kept(m):
        if m in FAR_FIRST:
            return ((1 - i1,),), ((i1, 1 - i2), (1 - i2,)), ((i1, i2), (i2,))
        return ((1 - i2,),), ((i2, 1 - i3), (1 - i3,)), ((i2, i3), (i3,))

    def remote(step, s, m):
        if step == 0:
            src, dst, dev = part.at[s, m, 1 - core], r_core.at[s, m], sibling
        elif step < 4:
            dev, place = leaving(m)[step - 1]
            src, dst = part.at[(s, m, core) + place], (r_one, r_two, r_three)[step - 1].at[s, m]
        else:
            dev, place = (sibling, ()) if step == 7 else returning(m)[step - 4]
            src = dst = full.at[(m, core, s) + place]
        return pltpu.make_async_remote_copy(
            src_ref=src,
            dst_ref=dst,
            send_sem=send_sem.at[step, s, m],
            recv_sem=recv_sem.at[step, s, m],
            device_id=dev,
            device_id_type=MESH,
        )

    def column(which, k, s=None):
        source, dz = SENDS.get(k, (0, 1))
        ref = (xs, ys)[which]
        target = at_col(k, -1) if source == 0 else (row, y_lo * 4 + (z - OFFSETS[k][1] + 4) % 4)
        slot = k if s is None else s
        return pltpu.make_async_remote_copy(
            src_ref=ref.at[pl.ds(source * rows, rows)],
            dst_ref=ref.at[pl.ds(pl.multiple_of(slot * rows, rows), rows)],
            send_sem=col_send.at[which, slot],
            recv_sem=col_recv.at[which, slot],
            device_id=target,
            device_id_type=MESH,
        )

    def dx_copy(k):
        return pltpu.make_async_remote_copy(
            src_ref=dx_send.at[k],
            dst_ref=dx_recv.at[k],
            send_sem=dx_ssem.at[k],
            recv_sem=dx_rsem.at[k],
            device_id=at_col(k, 1),
            device_id_type=MESH,
        )

    def local(i, src, dst):
        return pltpu.make_async_copy(src, dst, local_sem.at[i])

    def f32(v):
        return v.astype(jnp.float32)

    def gathered(which, s):
        @pl.when(s != 2)
        def _():
            column(which, 1, s).wait_recv()

        @pl.when(s == 1)
        def _():
            column(which, 1, 2).wait_recv()

        for at, ks in SEND_AT.items():

            @pl.when(s == at)
            def _():
                for k in ks:
                    column(which, k).start()

    def multiply(s, m):
        block = pl.ds(s * rows if isinstance(s, int) else pl.multiple_of(s * rows, rows), rows)
        for h in range(2):
            if m < 2:
                value = dot(xs[block, :], (wg, wu)[m][:, h * half : (h + 1) * half])
            else:
                value = dot(ys[block, :], wd[h * half : (h + 1) * half, :], NT)
            part[s, m, h] = value.astype(jnp.bfloat16).reshape(shape)

    def partials(s, m):
        if m != 1:
            gathered(m // 2, s)
        multiply(s, m)
        remote(0, s, m).start()

    def reduce(step, s, m):
        remote(step - 1, s, m).wait_recv()
        place = leaving(m)[step - 1][1]
        total = f32(part[(s, m, core) + place]) + f32(r_core[(s, m) + place])
        if step > 1:
            for ref, at in zip((r_one, r_two), kept(m)[step - 2]):
                total = total + f32(ref[(s, m) + at])
        part[(s, m, core) + place] = total.astype(jnp.bfloat16)
        remote(step, s, m).start()

    def activate(j):
        s = (j + 1) % BLOCKS
        sums = []
        for m in range(3):
            remote(3, s, m).wait_recv()
            total = f32(part[s, m, core, i1, i2, i3]) + f32(r_core[s, m, i1, i2, i3])
            for ref, at in zip((r_one, r_two), kept(m)[2]):
                total = total + f32(ref[(s, m) + at])
            total = total + f32(r_three[s, m])
            sums.append(f32(total.astype(jnp.bfloat16)))
        gate, up, grad = sums
        sig = 1.0 / (1.0 + jnp.exp(-gate))
        act = gate * sig
        out = (act * up, grad * up * sig * (1.0 + gate * (1.0 - sig)), grad * act)
        for m in range(3):
            full[m, core, j, i1, i2, i3] = out[m].astype(jnp.bfloat16)
            remote(4, j, m).start()

    def spread(step, j, m):
        remote(step - 1, j, m).wait_recv()
        remote(step, j, m).start()

    def input_grad(j):
        for m in range(3):
            remote(7, j, m).wait_recv()
        total = None
        for m, w in ((1, wg), (2, wu)):
            for h in range(2):
                values = full[m, h, j].reshape(rows, half)
                term = dot(values, w[:, h * half : (h + 1) * half], NT)
                total = term if total is None else total + term
        value = total.astype(jnp.bfloat16)

        @pl.when(j == BLOCKS - 1)
        def _():
            dx_recv[0] = value

        @pl.when(j < BLOCKS - 1)
        def _():
            dx_send[j + 1] = value

        for k in range(1, BLOCKS):

            @pl.when(j == k - 1)
            def _():
                dx_copy(k).start()

    def weight_part(p, q, closing=False):
        m, h = (1, 2, 0)[q // 2], q % 2
        pair = pl.ds(2 * p, 2)
        start = (2 * p + 1) * rows
        tokens = pl.ds(start if closing else pl.multiple_of(start, rows), 2 * rows)

        def put(acc, out, at, value):
            value = value + acc[at]
            if closing:
                out[at] = value.astype(jnp.bfloat16)
            else:
                acc[at] = value

        if m:
            acc, out = ((acc_gate, gate_out), (acc_up, up_out))[m - 1]
            values = full[m, h, pair].reshape(2 * rows, half)
            tile = 256
            for i in range(width // tile):
                r = slice(i * tile, (i + 1) * tile)
                put(acc, out, (r, slice(h * half, (h + 1) * half)), dot(xs[tokens, r], values, TN))
        else:
            tile = 128

            @pl.loop(0, half // tile)
            def _(i):
                r = pl.ds(pl.multiple_of(i * tile, tile), tile)
                values = full[0, h, pair, :, :, :, :, r].reshape(2 * rows, tile)
                at = pl.ds(pl.multiple_of(h * half + i * tile, tile), tile)
                put(acc_down, down_out, (at, slice(None)), dot(values, ys[tokens, :], TN))

    def weight_parts(j, i):
        @pl.when((j % 2 == 1) & (j < BLOCKS - 1))
        def _():
            weight_part(j // 2, i)

        @pl.when((j % 2 == 0) & (j > 0))
        def _():
            weight_part(j // 2 - 1, 3 + i)

    def work(stage, j, m):
        if stage == 0:
            partials(j, m)
        elif stage < 4:
            reduce(stage, j, m)
        elif stage == 4:
            activate(j)
        elif stage < 8:
            spread(stage, j, m)
        elif stage == 8:
            input_grad(j)
        else:
            weight_parts(j, m)

    loads = [
        local(0, x_in, xs.at[pl.ds(0, rows)]),
        local(1, y_in, ys.at[pl.ds(0, rows)]),
        local(5, x_in, xs.at[pl.ds(BLOCKS * rows, rows)]),
        local(6, y_in, ys.at[pl.ds(BLOCKS * rows, rows)]),
        local(2, gate_in, wg),
        local(3, up_in, wu),
        local(4, down_in, wd),
    ]
    for copy in loads:
        copy.start()

    barrier = pltpu.get_barrier_semaphore()
    partners = [sibling, first, second, far] + [at_col(k, 1) for k in range(1, BLOCKS)]
    for dev in partners:
        pl.semaphore_signal(barrier, inc=1, device_id=dev, device_id_type=MESH)
    for acc in (acc_gate, acc_up, acc_down):
        acc[...] = jnp.zeros_like(acc)
    loads[0].wait()
    loads[1].wait()
    pl.semaphore_wait(barrier, len(partners))
    for which in range(2):
        for k in (1, 2, 3):
            column(which, k).start()
    for copy in loads[2:]:
        copy.wait()
    for m in range(3):
        multiply(0, m)
        remote(0, 0, m).start()

    @pl.loop(0, BLOCKS + max(DELAYS))
    def _(t):
        for stage, items in itertools.groupby(ORDER, lambda item: item[0]):
            delay = DELAYS[stage]

            @pl.when((t >= delay + (stage == 0)) & (t < delay + BLOCKS))
            def _():
                for _, m in items:
                    work(stage, t - delay, m)

    for q in range(6):
        weight_part(BLOCKS // 2 - 1, q, True)
    total = f32(dx_recv[0])
    for k in range(1, BLOCKS):
        dx_copy(k).wait_recv()
        total = total + f32(dx_recv[k])
    gx_out[...] = total.astype(jnp.bfloat16)

    @pl.loop(0, BLOCKS)
    def _(s):
        for m in range(3):
            for step in range(8):
                remote(step, s, m).wait_send()

    for k in range(1, BLOCKS):
        column(0, k).wait_send()
        column(1, k).wait_send()
        dx_copy(k).wait_send()


def place_kernel(*refs):
    sem = refs[-1]
    count = len(refs) // 2
    copies = [pltpu.make_async_copy(refs[i], refs[count + i], sem.at[i]) for i in range(count)]
    for copy in copies:
        copy.start()
    for copy in copies:
        copy.wait()


def on_device(inputs, cotangent, gate_weight, up_weight, down_weight):
    rows, width = inputs.shape
    columns = gate_weight.shape[1]
    half, tokens = columns // 2, rows * BLOCKS
    bf16 = jnp.bfloat16
    block = (2, 2, 2, rows // 8)
    anywhere = pl.BlockSpec(memory_space=pl.ANY)
    inside = pl.BlockSpec(memory_space=pltpu.VMEM)
    dma = pltpu.SemaphoreType.DMA
    results = [jax.ShapeDtypeStruct(a.shape, bf16) for a in (inputs, gate_weight, up_weight, down_weight)]
    grads = pl.pallas_call(
        exchange_kernel,
        out_shape=[pltpu.VMEM(a.shape, bf16) for a in results],
        in_specs=[anywhere] * 5,
        out_specs=[inside] * 4,
        scratch_shapes=[
            pltpu.VMEM((tokens + rows, width), bf16),
            pltpu.VMEM((tokens + rows, width), bf16),
            pltpu.VMEM((width, columns), bf16),
            pltpu.VMEM((width, columns), bf16),
            pltpu.VMEM((columns, width), bf16),
            pltpu.VMEM((BLOCKS, 3, 2, *block, half), bf16),
            pltpu.VMEM((BLOCKS, 3, *block, half), bf16),
            pltpu.VMEM((BLOCKS, 3, *block[1:], half), bf16),
            pltpu.VMEM((BLOCKS, 3, *block[2:], half), bf16),
            pltpu.VMEM((BLOCKS, 3, *block[3:], half), bf16),
            pltpu.VMEM((3, 2, BLOCKS, *block, half), bf16),
            pltpu.VMEM((width, columns), jnp.float32),
            pltpu.VMEM((width, columns), jnp.float32),
            pltpu.VMEM((columns, width), jnp.float32),
            pltpu.VMEM((BLOCKS, rows, width), bf16),
            pltpu.VMEM((BLOCKS, rows, width), bf16),
            dma((7,)),
            dma((8, BLOCKS, 3)),
            dma((8, BLOCKS, 3)),
            dma((2, BLOCKS)),
            dma((2, BLOCKS)),
            dma((BLOCKS,)),
            dma((BLOCKS,)),
        ],
        compiler_params=pltpu.CompilerParams(
            collective_id=0, has_side_effects=True, vmem_limit_bytes=56 * 1024 * 1024
        ),
        cost_estimate=pl.CostEstimate(
            flops=16 * tokens * width * columns, bytes_accessed=24_000_000, transcendentals=0
        ),
    )(inputs, cotangent, gate_weight, up_weight, down_weight)

    return pl.pallas_call(
        place_kernel,
        out_shape=results,
        in_specs=[inside] * 4,
        out_specs=[anywhere] * 4,
        scratch_shapes=[dma((4,))],
        compiler_params=pltpu.CompilerParams(vmem_limit_bytes=1024 * 1024),
        cost_estimate=pl.CostEstimate(flops=0, bytes_accessed=12_000_000, transcendentals=0),
    )(*grads)


def solution(mesh):
    placed = (P("col", "row"), P("col", "row"), P("row", "col"), P("row", "col"), P("col", "row"))
    return jax.shard_map(
        on_device,
        mesh=mesh,
        in_specs=placed,
        out_specs=(P("col", "row"), P("row", "col"), P("row", "col"), P("col", "row")),
        check_vma=False,
    )
```

```python
import itertools

import jax
import jax.numpy as jnp
from jax import lax
from jax.experimental import pallas as pl
from jax.experimental.pallas import tpu as pltpu
from jax.sharding import PartitionSpec as P

MESH = pl.DeviceIdType.MESH
BLOCKS = 8
OFFSETS = ((0, 0), (0, 1), (1, 0), (0, 3), (1, 1), (1, 3), (0, 2), (1, 2))
SENDS = {1: (0, 1), 2: (0, 0), 3: (0, 3), 4: (2, 1), 5: (2, 3), 6: (0, 2), 7: (2, 2)}
SEND_AT = {1: (4, 5), 2: (6,), 3: (7,)}
DELAYS = (0, 1, 3, 5, 8, 9, 12, 14, 15, 15)
ORDER = ((4, 0), (2, 0), (2, 1), (6, 0), (6, 1), (3, 0), (3, 1), (1, 0), (1, 1), (8, 0), (7, 0), (7, 1), (9, 0), (9, 1), (9, 2), (5, 0), (5, 1), (0, 0), (0, 1))
UNITS = (slice(0, 2), slice(2, 3))
FAR_FIRST = (1,)
FAR_LAST = (1,)
NT = (((1,), (1,)), ((), ()))
TN = (((0,), (0,)), ((), ()))


def dot(a, b, dims=(((1,), (0,)), ((), ()))):
    return lax.dot_general(a, b, dims, preferred_element_type=jnp.float32)


def exchange_kernel(
    x_in, y_in, gate_in, up_in, down_in,
    gx_out, gate_out, up_out, down_out,
    xs, ys, wg, wu, wd, part, r_core, r_one, r_two, r_three, full, acc_gate, acc_up, acc_down,
    dx_send, dx_recv, local_sem, send_sem, recv_sem, col_send, col_recv, dx_ssem, dx_rsem,
):
    rows, width = x_in.shape
    half = gate_in.shape[1] // 2
    shape = part.shape[3:]
    row, col = lax.axis_index("row"), lax.axis_index("col")
    core, y_hi, x = row % 2, (row // 2) % 2, row // 4
    y_lo, z = col // 4, col % 4
    bit_a, bit_b = x // 2, (x + x // 2) % 2
    flip_a, flip_b = 3 - x, x + 1 - 2 * (x % 2)
    i1 = core * bit_a + (1 - core) * bit_b
    i2 = core * bit_b + (1 - core) * bit_a
    i3 = y_hi
    x1 = core * flip_a + (1 - core) * flip_b
    x2 = core * flip_b + (1 - core) * flip_a
    sibling = (row + 1 - 2 * core, col)
    first = (x1 * 4 + y_hi * 2 + core, col)
    second = (x2 * 4 + y_hi * 2 + core, col)
    far = (x * 4 + (1 - y_hi) * 2 + core, col)
    every = slice(None)

    def at_col(k, sign):
        dy, dz = OFFSETS[k]
        return (row, (1 - y_lo if dy else y_lo) * 4 + (z + sign * dz + 4) % 4)

    def leaving(u):
        if u in FAR_FIRST:
            return (far, (every, every, 1 - i3)), (first, (1 - i1, every, i3)), (second, (i1, 1 - i2, i3))
        return (first, (1 - i1,)), (second, (i1, 1 - i2)), (far, (i1, i2, 1 - i3))

    def returning(u):
        if u in FAR_LAST:
            return (second, (i1, i2, i3)), (first, (i1, every, i3)), (far, (every, every, i3))
        return (far, (i1, i2, i3)), (second, (i1, i2)), (first, (i1,))

    def kept(u):
        if u in FAR_FIRST:
            return ((1 - i1,),), ((i1, 1 - i2), (1 - i2,)), ((i1, i2), (i2,))
        return ((1 - i2,),), ((i2, 1 - i3), (1 - i3,)), ((i2, i3), (i3,))

    def remote(step, s, u):
        ms = UNITS[u]
        if step == 0:
            src, dst, dev = part.at[s, ms, 1 - core], r_core.at[s, ms], sibling
        elif step < 4:
            dev, place = leaving(u)[step - 1]
            src, dst = part.at[(s, ms, core) + place], (r_one, r_two, r_three)[step - 1].at[s, ms]
        else:
            dev, place = (sibling, ()) if step == 7 else returning(u)[step - 4]
            src = dst = full.at[(ms, core, s) + place]
        return pltpu.make_async_remote_copy(
            src_ref=src,
            dst_ref=dst,
            send_sem=send_sem.at[step, s, u],
            recv_sem=recv_sem.at[step, s, u],
            device_id=dev,
            device_id_type=MESH,
        )

    def column(which, k, s=None):
        source, dz = SENDS.get(k, (0, 1))
        ref = (xs, ys)[which]
        target = at_col(k, -1) if source == 0 else (row, y_lo * 4 + (z - OFFSETS[k][1] + 4) % 4)
        slot = k if s is None else s
        return pltpu.make_async_remote_copy(
            src_ref=ref.at[pl.ds(source * rows, rows)],
            dst_ref=ref.at[pl.ds(pl.multiple_of(slot * rows, rows), rows)],
            send_sem=col_send.at[which, slot],
            recv_sem=col_recv.at[which, slot],
            device_id=target,
            device_id_type=MESH,
        )

    def dx_copy(k):
        return pltpu.make_async_remote_copy(
            src_ref=dx_send.at[k],
            dst_ref=dx_recv.at[k],
            send_sem=dx_ssem.at[k],
            recv_sem=dx_rsem.at[k],
            device_id=at_col(k, 1),
            device_id_type=MESH,
        )

    def local(i, src, dst):
        return pltpu.make_async_copy(src, dst, local_sem.at[i])

    def f32(v):
        return v.astype(jnp.float32)

    def gathered(which, s):
        @pl.when(s != 2)
        def _():
            column(which, 1, s).wait_recv()

        @pl.when(s == 1)
        def _():
            column(which, 1, 2).wait_recv()

        for at, ks in SEND_AT.items():

            @pl.when(s == at)
            def _():
                for k in ks:
                    column(which, k).start()

    def multiply(s, m):
        block = pl.ds(s * rows if isinstance(s, int) else pl.multiple_of(s * rows, rows), rows)
        for h in range(2):
            if m < 2:
                value = dot(xs[block, :], (wg, wu)[m][:, h * half : (h + 1) * half])
            else:
                value = dot(ys[block, :], wd[h * half : (h + 1) * half, :], NT)
            part[s, m, h] = value.astype(jnp.bfloat16).reshape(shape)

    def partials(s, u):
        gathered(u, s)
        for m in range(UNITS[u].start, UNITS[u].stop):
            multiply(s, m)
        remote(0, s, u).start()

    def reduce(step, s, u):
        remote(step - 1, s, u).wait_recv()
        ms, place = UNITS[u], leaving(u)[step - 1][1]
        total = f32(part[(s, ms, core) + place]) + f32(r_core[(s, ms) + place])
        if step > 1:
            for ref, at in zip((r_one, r_two), kept(u)[step - 2]):
                total = total + f32(ref[(s, ms) + at])
        part[(s, ms, core) + place] = total.astype(jnp.bfloat16)
        remote(step, s, u).start()

    def activate(j):
        s = (j + 1) % BLOCKS
        sums = []
        for u, ms in enumerate(UNITS):
            remote(3, s, u).wait_recv()
            for m in range(ms.start, ms.stop):
                total = f32(part[s, m, core, i1, i2, i3]) + f32(r_core[s, m, i1, i2, i3])
                for ref, at in zip((r_one, r_two), kept(u)[2]):
                    total = total + f32(ref[(s, m) + at])
                total = total + f32(r_three[s, m])
                sums.append(f32(total.astype(jnp.bfloat16)))
        gate, up, grad = sums
        sig = 1.0 / (1.0 + jnp.exp(-gate))
        act = gate * sig
        out = (act * up, grad * up * sig * (1.0 + gate * (1.0 - sig)), grad * act)
        for u, ms in enumerate(UNITS):
            for m in range(ms.start, ms.stop):
                full[m, core, j, i1, i2, i3] = out[m].astype(jnp.bfloat16)
            remote(4, j, u).start()

    def spread(step, j, u):
        remote(step - 1, j, u).wait_recv()
        remote(step, j, u).start()

    def input_grad(j):
        for u in range(len(UNITS)):
            remote(7, j, u).wait_recv()
        total = None
        for m, w in ((1, wg), (2, wu)):
            for h in range(2):
                values = full[m, h, j].reshape(rows, half)
                term = dot(values, w[:, h * half : (h + 1) * half], NT)
                total = term if total is None else total + term
        value = total.astype(jnp.bfloat16)

        @pl.when(j == BLOCKS - 1)
        def _():
            dx_recv[0] = value

        @pl.when(j < BLOCKS - 1)
        def _():
            dx_send[j + 1] = value

        for k in range(1, BLOCKS):

            @pl.when(j == k - 1)
            def _():
                dx_copy(k).start()

    def weight_part(p, q, closing=False):
        m, h = (1, 2, 0)[q // 2], q % 2
        pair = pl.ds(2 * p, 2)
        start = (2 * p + 1) * rows
        tokens = pl.ds(start if closing else pl.multiple_of(start, rows), 2 * rows)

        def put(acc, out, at, value):
            value = value + acc[at]
            if closing:
                out[at] = value.astype(jnp.bfloat16)
            else:
                acc[at] = value

        if m:
            acc, out = ((acc_gate, gate_out), (acc_up, up_out))[m - 1]
            values = full[m, h, pair].reshape(2 * rows, half)
            tile = 256
            for i in range(width // tile):
                r = slice(i * tile, (i + 1) * tile)
                put(acc, out, (r, slice(h * half, (h + 1) * half)), dot(xs[tokens, r], values, TN))
        else:
            tile = 128

            @pl.loop(0, half // tile)
            def _(i):
                r = pl.ds(pl.multiple_of(i * tile, tile), tile)
                values = full[0, h, pair, :, :, :, :, r].reshape(2 * rows, tile)
                at = pl.ds(pl.multiple_of(h * half + i * tile, tile), tile)
                put(acc_down, down_out, (at, slice(None)), dot(values, ys[tokens, :], TN))

    def weight_parts(j, i):
        @pl.when((j % 2 == 1) & (j < BLOCKS - 1))
        def _():
            weight_part(j // 2, i)

        @pl.when((j % 2 == 0) & (j > 0))
        def _():
            weight_part(j // 2 - 1, 3 + i)

    def work(stage, j, m):
        if stage == 0:
            partials(j, m)
        elif stage < 4:
            reduce(stage, j, m)
        elif stage == 4:
            activate(j)
        elif stage < 8:
            spread(stage, j, m)
        elif stage == 8:
            input_grad(j)
        else:
            weight_parts(j, m)

    loads = [
        local(0, x_in, xs.at[pl.ds(0, rows)]),
        local(1, y_in, ys.at[pl.ds(0, rows)]),
        local(5, x_in, xs.at[pl.ds(BLOCKS * rows, rows)]),
        local(6, y_in, ys.at[pl.ds(BLOCKS * rows, rows)]),
        local(2, gate_in, wg),
        local(3, up_in, wu),
        local(4, down_in, wd),
    ]
    for copy in loads:
        copy.start()

    barrier = pltpu.get_barrier_semaphore()
    partners = [sibling, first, second, far] + [at_col(k, 1) for k in range(1, BLOCKS)]
    for dev in partners:
        pl.semaphore_signal(barrier, inc=1, device_id=dev, device_id_type=MESH)
    for acc in (acc_gate, acc_up, acc_down):
        acc[...] = jnp.zeros_like(acc)
    loads[0].wait()
    loads[1].wait()
    pl.semaphore_wait(barrier, len(partners))
    for which in range(2):
        for k in (1, 2, 3):
            column(which, k).start()
    for copy in loads[2:]:
        copy.wait()
    for u, ms in enumerate(UNITS):
        for m in range(ms.start, ms.stop):
            multiply(0, m)
        remote(0, 0, u).start()

    @pl.loop(0, BLOCKS + max(DELAYS))
    def _(t):
        for stage, items in itertools.groupby(ORDER, lambda item: item[0]):
            delay = DELAYS[stage]

            @pl.when((t >= delay + (stage == 0)) & (t < delay + BLOCKS))
            def _():
                for _, m in items:
                    work(stage, t - delay, m)

    for q in range(6):
        weight_part(BLOCKS // 2 - 1, q, True)
    total = f32(dx_recv[0])
    for k in range(1, BLOCKS):
        dx_copy(k).wait_recv()
        total = total + f32(dx_recv[k])
    gx_out[...] = total.astype(jnp.bfloat16)

    @pl.loop(0, BLOCKS)
    def _(s):
        for u in range(len(UNITS)):
            for step in range(8):
                remote(step, s, u).wait_send()

    for k in range(1, BLOCKS):
        column(0, k).wait_send()
        column(1, k).wait_send()
        dx_copy(k).wait_send()


def place_kernel(*refs):
    sem = refs[-1]
    count = len(refs) // 2
    copies = [pltpu.make_async_copy(refs[i], refs[count + i], sem.at[i]) for i in range(count)]
    for copy in copies:
        copy.start()
    for copy in copies:
        copy.wait()


def on_device(inputs, cotangent, gate_weight, up_weight, down_weight):
    rows, width = inputs.shape
    columns = gate_weight.shape[1]
    half, tokens = columns // 2, rows * BLOCKS
    bf16 = jnp.bfloat16
    block = (2, 2, 2, rows // 8)
    anywhere = pl.BlockSpec(memory_space=pl.ANY)
    inside = pl.BlockSpec(memory_space=pltpu.VMEM)
    dma = pltpu.SemaphoreType.DMA
    results = [jax.ShapeDtypeStruct(a.shape, bf16) for a in (inputs, gate_weight, up_weight, down_weight)]
    grads = pl.pallas_call(
        exchange_kernel,
        out_shape=[pltpu.VMEM(a.shape, bf16) for a in results],
        in_specs=[anywhere] * 5,
        out_specs=[inside] * 4,
        scratch_shapes=[
            pltpu.VMEM((tokens + rows, width), bf16),
            pltpu.VMEM((tokens + rows, width), bf16),
            pltpu.VMEM((width, columns), bf16),
            pltpu.VMEM((width, columns), bf16),
            pltpu.VMEM((columns, width), bf16),
            pltpu.VMEM((BLOCKS, 3, 2, *block, half), bf16),
            pltpu.VMEM((BLOCKS, 3, *block, half), bf16),
            pltpu.VMEM((BLOCKS, 3, *block[1:], half), bf16),
            pltpu.VMEM((BLOCKS, 3, *block[2:], half), bf16),
            pltpu.VMEM((BLOCKS, 3, *block[3:], half), bf16),
            pltpu.VMEM((3, 2, BLOCKS, *block, half), bf16),
            pltpu.VMEM((width, columns), jnp.float32),
            pltpu.VMEM((width, columns), jnp.float32),
            pltpu.VMEM((columns, width), jnp.float32),
            pltpu.VMEM((BLOCKS, rows, width), bf16),
            pltpu.VMEM((BLOCKS, rows, width), bf16),
            dma((7,)),
            dma((8, BLOCKS, 2)),
            dma((8, BLOCKS, 2)),
            dma((2, BLOCKS)),
            dma((2, BLOCKS)),
            dma((BLOCKS,)),
            dma((BLOCKS,)),
        ],
        compiler_params=pltpu.CompilerParams(
            collective_id=0, has_side_effects=True, vmem_limit_bytes=56 * 1024 * 1024
        ),
        cost_estimate=pl.CostEstimate(
            flops=16 * tokens * width * columns, bytes_accessed=24_000_000, transcendentals=0
        ),
    )(inputs, cotangent, gate_weight, up_weight, down_weight)

    return pl.pallas_call(
        place_kernel,
        out_shape=results,
        in_specs=[inside] * 4,
        out_specs=[anywhere] * 4,
        scratch_shapes=[dma((4,))],
        compiler_params=pltpu.CompilerParams(vmem_limit_bytes=1024 * 1024),
        cost_estimate=pl.CostEstimate(flops=0, bytes_accessed=12_000_000, transcendentals=0),
    )(*grads)


def solution(mesh):
    placed = (P("col", "row"), P("col", "row"), P("row", "col"), P("row", "col"), P("col", "row"))
    return jax.shard_map(
        on_device,
        mesh=mesh,
        in_specs=placed,
        out_specs=(P("col", "row"), P("row", "col"), P("row", "col"), P("col", "row")),
        check_vma=False,
    )
```

```python
import itertools

import jax
import jax.numpy as jnp
from jax import lax
from jax.experimental import pallas as pl
from jax.experimental.pallas import tpu as pltpu
from jax.sharding import PartitionSpec as P

MESH = pl.DeviceIdType.MESH
BLOCKS = 8
OFFSETS = ((0, 0), (0, 1), (1, 0), (0, 3), (1, 1), (1, 3), (0, 2), (1, 2))
SENDS = {1: (0, 1), 2: (0, 0), 3: (0, 3), 4: (2, 1), 5: (2, 3), 6: (0, 2), 7: (2, 2)}
SEND_AT = {1: (4, 5), 2: (6,), 3: (7,)}
DELAYS = (0, 1, 3, 5, 8, 9, 12, 14, 15, 15)
ORDER = ((4, 0), (2, 0), (2, 1), (6, 0), (6, 1), (3, 0), (3, 1), (1, 0), (1, 1), (8, 0), (7, 0), (7, 1), (9, 0), (9, 1), (9, 2), (5, 0), (5, 1), (0, 0), (0, 1))
UNITS = (slice(0, 2), slice(2, 3))
FAR_FIRST = (1,)
FAR_LAST = (1,)
NT = (((1,), (1,)), ((), ()))
TN = (((0,), (0,)), ((), ()))


def dot(a, b, dims=(((1,), (0,)), ((), ()))):
    return lax.dot_general(a, b, dims, preferred_element_type=jnp.float32)


def exchange_kernel(
    x_in, y_in, gate_in, up_in, down_in,
    gx_out, gate_out, up_out, down_out,
    xs, ys, wg, wu, wd, part, r_core, r_one, r_two, r_three, full, acc_gate, acc_up, acc_down,
    dx_send, dx_recv, local_sem, send_sem, recv_sem, col_send, col_recv, dx_ssem, dx_rsem,
):
    rows, width = x_in.shape
    half = gate_in.shape[1] // 2
    shape = part.shape[3:]
    row, col = lax.axis_index("row"), lax.axis_index("col")
    core, y_hi, x = row % 2, (row // 2) % 2, row // 4
    y_lo, z = col // 4, col % 4
    bit_a, bit_b = x // 2, (x + x // 2) % 2
    flip_a, flip_b = 3 - x, x + 1 - 2 * (x % 2)
    i1 = core * bit_a + (1 - core) * bit_b
    i2 = core * bit_b + (1 - core) * bit_a
    i3 = y_hi
    x1 = core * flip_a + (1 - core) * flip_b
    x2 = core * flip_b + (1 - core) * flip_a
    sibling = (row + 1 - 2 * core, col)
    first = (x1 * 4 + y_hi * 2 + core, col)
    second = (x2 * 4 + y_hi * 2 + core, col)
    far = (x * 4 + (1 - y_hi) * 2 + core, col)
    every = slice(None)

    def at_col(k, sign):
        dy, dz = OFFSETS[k]
        return (row, (1 - y_lo if dy else y_lo) * 4 + (z + sign * dz + 4) % 4)

    def leaving(u):
        if u in FAR_FIRST:
            return (far, (every, every, 1 - i3)), (first, (1 - i1, every, i3)), (second, (i1, 1 - i2, i3))
        return (first, (1 - i1,)), (second, (i1, 1 - i2)), (far, (i1, i2, 1 - i3))

    def returning(u):
        if u in FAR_LAST:
            return (second, (i1, i2, i3)), (first, (i1, every, i3)), (far, (every, every, i3))
        return (far, (i1, i2, i3)), (second, (i1, i2)), (first, (i1,))

    def kept(u):
        if u in FAR_FIRST:
            return ((1 - i1,),), ((i1, 1 - i2), (1 - i2,)), ((i1, i2), (i2,))
        return ((1 - i2,),), ((i2, 1 - i3), (1 - i3,)), ((i2, i3), (i3,))

    def remote(step, s, u):
        ms = UNITS[u]
        if step == 0:
            src, dst, dev = part.at[s, ms, 1 - core], r_core.at[s, ms], sibling
        elif step < 4:
            dev, place = leaving(u)[step - 1]
            src, dst = part.at[(s, ms, core) + place], (r_one, r_two, r_three)[step - 1].at[s, ms]
        else:
            dev, place = (sibling, ()) if step == 7 else returning(u)[step - 4]
            src = dst = full.at[(ms, core, s) + place]
        return pltpu.make_async_remote_copy(
            src_ref=src,
            dst_ref=dst,
            send_sem=send_sem.at[step, s, u],
            recv_sem=recv_sem.at[step, s, u],
            device_id=dev,
            device_id_type=MESH,
        )

    def column(which, k, s=None):
        source, dz = SENDS.get(k, (0, 1))
        ref = (xs, ys)[which]
        target = at_col(k, -1) if source == 0 else (row, y_lo * 4 + (z - OFFSETS[k][1] + 4) % 4)
        slot = k if s is None else s
        return pltpu.make_async_remote_copy(
            src_ref=ref.at[pl.ds(source * rows, rows)],
            dst_ref=ref.at[pl.ds(pl.multiple_of(slot * rows, rows), rows)],
            send_sem=col_send.at[which, slot],
            recv_sem=col_recv.at[which, slot],
            device_id=target,
            device_id_type=MESH,
        )

    def dx_copy(k):
        return pltpu.make_async_remote_copy(
            src_ref=dx_send.at[k],
            dst_ref=dx_recv.at[k],
            send_sem=dx_ssem.at[k],
            recv_sem=dx_rsem.at[k],
            device_id=at_col(k, 1),
            device_id_type=MESH,
        )

    def local(i, src, dst):
        return pltpu.make_async_copy(src, dst, local_sem.at[i])

    def f32(v):
        return v.astype(jnp.float32)

    def gathered(which, s):
        @pl.when(s != 2)
        def _():
            column(which, 1, s).wait_recv()

        @pl.when(s == 1)
        def _():
            column(which, 1, 2).wait_recv()

        for at, ks in SEND_AT.items():

            @pl.when(s == at)
            def _():
                for k in ks:
                    column(which, k).start()

    def multiply(s, m):
        block = pl.ds(s * rows if isinstance(s, int) else pl.multiple_of(s * rows, rows), rows)
        for h in range(2):
            if m < 2:
                value = dot(xs[block, :], (wg, wu)[m][:, h * half : (h + 1) * half])
            else:
                value = dot(ys[block, :], wd[h * half : (h + 1) * half, :], NT)
            part[s, m, h] = value.astype(jnp.bfloat16).reshape(shape)

    def partials(s, u):
        gathered(u, s)
        for m in range(UNITS[u].start, UNITS[u].stop):
            multiply(s, m)
        remote(0, s, u).start()

    def reduce(step, s, u):
        remote(step - 1, s, u).wait_recv()
        ms, place = UNITS[u], leaving(u)[step - 1][1]
        total = f32(part[(s, ms, core) + place]) + f32(r_core[(s, ms) + place])
        if step > 1:
            for ref, at in zip((r_one, r_two), kept(u)[step - 2]):
                total = total + f32(ref[(s, ms) + at])
        part[(s, ms, core) + place] = total.astype(jnp.bfloat16)
        remote(step, s, u).start()

    def activate(j):
        s = (j + 1) % BLOCKS
        sums = []
        for u, ms in enumerate(UNITS):
            remote(3, s, u).wait_recv()
            for m in range(ms.start, ms.stop):
                total = f32(part[s, m, core, i1, i2, i3]) + f32(r_core[s, m, i1, i2, i3])
                for ref, at in zip((r_one, r_two), kept(u)[2]):
                    total = total + f32(ref[(s, m) + at])
                total = total + f32(r_three[s, m])
                sums.append(f32(total.astype(jnp.bfloat16)))
        gate, up, grad = sums
        sig = 1.0 / (1.0 + jnp.exp(-gate))
        act = gate * sig
        out = (act * up, grad * up * sig * (1.0 + gate * (1.0 - sig)), grad * act)
        for u, ms in enumerate(UNITS):
            for m in range(ms.start, ms.stop):
                full[m, core, j, i1, i2, i3] = out[m].astype(jnp.bfloat16)
            remote(4, j, u).start()

    def spread(step, j, u):
        remote(step - 1, j, u).wait_recv()
        remote(step, j, u).start()

    def close(h):
        for q in (0, 2, 4):
            weight_part(BLOCKS // 2 - 1, q, True, h)

    def input_grad(j):
        @pl.when(j == BLOCKS - 1)
        def _():
            close(core)

        for u in range(len(UNITS)):
            remote(7, j, u).wait_recv()
        total = None
        for m, w in ((1, wg), (2, wu)):
            for h in range(2):
                values = full[m, h, j].reshape(rows, half)
                term = dot(values, w[:, h * half : (h + 1) * half], NT)
                total = term if total is None else total + term
        value = total.astype(jnp.bfloat16)

        @pl.when(j == BLOCKS - 1)
        def _():
            dx_recv[0] = value

        @pl.when(j < BLOCKS - 1)
        def _():
            dx_send[j + 1] = value

        for k in range(1, BLOCKS):

            @pl.when(j == k - 1)
            def _():
                dx_copy(k).start()

    def weight_part(p, q, closing=False, h=None):
        m, h = (1, 2, 0)[q // 2], q % 2 if h is None else h
        here = pl.ds(h * half if isinstance(h, int) else pl.multiple_of(h * half, 128), half)
        pair = pl.ds(2 * p, 2)
        start = (2 * p + 1) * rows
        tokens = pl.ds(start if closing else pl.multiple_of(start, rows), 2 * rows)

        def put(acc, out, at, value):
            value = value + acc[at]
            if closing:
                out[at] = value.astype(jnp.bfloat16)
            else:
                acc[at] = value

        if m:
            acc, out = ((acc_gate, gate_out), (acc_up, up_out))[m - 1]
            values = full[m, h, pair].reshape(2 * rows, half)
            tile = 256
            for i in range(width // tile):
                r = slice(i * tile, (i + 1) * tile)
                put(acc, out, (r, here), dot(xs[tokens, r], values, TN))
        else:
            tile = 128

            @pl.loop(0, half // tile)
            def _(i):
                r = pl.ds(pl.multiple_of(i * tile, tile), tile)
                values = full[0, h, pair, :, :, :, :, r].reshape(2 * rows, tile)
                at = pl.ds(pl.multiple_of(h * half + i * tile, tile), tile)
                put(acc_down, down_out, (at, slice(None)), dot(values, ys[tokens, :], TN))

    def weight_parts(j, i):
        @pl.when((j % 2 == 1) & (j < BLOCKS - 1))
        def _():
            weight_part(j // 2, i)

        @pl.when((j % 2 == 0) & (j > 0))
        def _():
            weight_part(j // 2 - 1, 3 + i)

    def work(stage, j, m):
        if stage == 0:
            partials(j, m)
        elif stage < 4:
            reduce(stage, j, m)
        elif stage == 4:
            activate(j)
        elif stage < 8:
            spread(stage, j, m)
        elif stage == 8:
            input_grad(j)
        else:
            weight_parts(j, m)

    loads = [
        local(0, x_in, xs.at[pl.ds(0, rows)]),
        local(1, y_in, ys.at[pl.ds(0, rows)]),
        local(5, x_in, xs.at[pl.ds(BLOCKS * rows, rows)]),
        local(6, y_in, ys.at[pl.ds(BLOCKS * rows, rows)]),
        local(2, gate_in, wg),
        local(3, up_in, wu),
        local(4, down_in, wd),
    ]
    for copy in loads:
        copy.start()

    barrier = pltpu.get_barrier_semaphore()
    partners = [sibling, first, second, far] + [at_col(k, 1) for k in range(1, BLOCKS)]
    for dev in partners:
        pl.semaphore_signal(barrier, inc=1, device_id=dev, device_id_type=MESH)
    for acc in (acc_gate, acc_up, acc_down):
        acc[...] = jnp.zeros_like(acc)
    loads[0].wait()
    loads[1].wait()
    pl.semaphore_wait(barrier, len(partners))
    for which in range(2):
        for k in (1, 2, 3):
            column(which, k).start()
    for copy in loads[2:]:
        copy.wait()
    for u, ms in enumerate(UNITS):
        for m in range(ms.start, ms.stop):
            multiply(0, m)
        remote(0, 0, u).start()

    @pl.loop(0, BLOCKS + max(DELAYS))
    def _(t):
        for stage, items in itertools.groupby(ORDER, lambda item: item[0]):
            delay = DELAYS[stage]

            @pl.when((t >= delay + (stage == 0)) & (t < delay + BLOCKS))
            def _():
                for _, m in items:
                    work(stage, t - delay, m)

    close(1 - core)
    total = f32(dx_recv[0])
    for k in range(1, BLOCKS):
        dx_copy(k).wait_recv()
        total = total + f32(dx_recv[k])
    gx_out[...] = total.astype(jnp.bfloat16)

    @pl.loop(0, BLOCKS)
    def _(s):
        for u in range(len(UNITS)):
            for step in range(8):
                remote(step, s, u).wait_send()

    for k in range(1, BLOCKS):
        column(0, k).wait_send()
        column(1, k).wait_send()
        dx_copy(k).wait_send()


def place_kernel(*refs):
    sem = refs[-1]
    count = len(refs) // 2
    copies = [pltpu.make_async_copy(refs[i], refs[count + i], sem.at[i]) for i in range(count)]
    for copy in copies:
        copy.start()
    for copy in copies:
        copy.wait()


def on_device(inputs, cotangent, gate_weight, up_weight, down_weight):
    rows, width = inputs.shape
    columns = gate_weight.shape[1]
    half, tokens = columns // 2, rows * BLOCKS
    bf16 = jnp.bfloat16
    block = (2, 2, 2, rows // 8)
    anywhere = pl.BlockSpec(memory_space=pl.ANY)
    inside = pl.BlockSpec(memory_space=pltpu.VMEM)
    dma = pltpu.SemaphoreType.DMA
    results = [jax.ShapeDtypeStruct(a.shape, bf16) for a in (inputs, gate_weight, up_weight, down_weight)]
    grads = pl.pallas_call(
        exchange_kernel,
        out_shape=[pltpu.VMEM(a.shape, bf16) for a in results],
        in_specs=[anywhere] * 5,
        out_specs=[inside] * 4,
        scratch_shapes=[
            pltpu.VMEM((tokens + rows, width), bf16),
            pltpu.VMEM((tokens + rows, width), bf16),
            pltpu.VMEM((width, columns), bf16),
            pltpu.VMEM((width, columns), bf16),
            pltpu.VMEM((columns, width), bf16),
            pltpu.VMEM((BLOCKS, 3, 2, *block, half), bf16),
            pltpu.VMEM((BLOCKS, 3, *block, half), bf16),
            pltpu.VMEM((BLOCKS, 3, *block[1:], half), bf16),
            pltpu.VMEM((BLOCKS, 3, *block[2:], half), bf16),
            pltpu.VMEM((BLOCKS, 3, *block[3:], half), bf16),
            pltpu.VMEM((3, 2, BLOCKS, *block, half), bf16),
            pltpu.VMEM((width, columns), jnp.float32),
            pltpu.VMEM((width, columns), jnp.float32),
            pltpu.VMEM((columns, width), jnp.float32),
            pltpu.VMEM((BLOCKS, rows, width), bf16),
            pltpu.VMEM((BLOCKS, rows, width), bf16),
            dma((7,)),
            dma((8, BLOCKS, 2)),
            dma((8, BLOCKS, 2)),
            dma((2, BLOCKS)),
            dma((2, BLOCKS)),
            dma((BLOCKS,)),
            dma((BLOCKS,)),
        ],
        compiler_params=pltpu.CompilerParams(
            collective_id=0, has_side_effects=True, vmem_limit_bytes=56 * 1024 * 1024
        ),
        cost_estimate=pl.CostEstimate(
            flops=16 * tokens * width * columns, bytes_accessed=24_000_000, transcendentals=0
        ),
    )(inputs, cotangent, gate_weight, up_weight, down_weight)

    return pl.pallas_call(
        place_kernel,
        out_shape=results,
        in_specs=[inside] * 4,
        out_specs=[anywhere] * 4,
        scratch_shapes=[dma((4,))],
        compiler_params=pltpu.CompilerParams(vmem_limit_bytes=1024 * 1024),
        cost_estimate=pl.CostEstimate(flops=0, bytes_accessed=12_000_000, transcendentals=0),
    )(*grads)


def solution(mesh):
    placed = (P("col", "row"), P("col", "row"), P("row", "col"), P("row", "col"), P("col", "row"))
    return jax.shard_map(
        on_device,
        mesh=mesh,
        in_specs=placed,
        out_specs=(P("col", "row"), P("row", "col"), P("row", "col"), P("col", "row")),
        check_vma=False,
    )
```
